32 devices in a mesh: fsdp: 32 (over z, y, x, core).
Axes of the slice: x: 2, y: 2, z: 4, core: 2. Of those that a mesh axis runs over, the one named last changes fastest.
Arguments:
- hidden_in: bfloat16 [32768, 768], P('fsdp'), may hold values from -6 to 6
- lengths: int32 [32], P('fsdp'), may hold values from 512 to 1024, as said below
- ln1_gain: bfloat16 [768], P('fsdp'), may hold values from 0.5 to 1.5
- ln1_bias: bfloat16 [768], P('fsdp'), may hold values from -1.75 to 1.75
- w_qkv: bfloat16 [768, 2304], P('fsdp'), may hold values from -0.3125 to 0.3125
- b_qv: bfloat16 [1536], P('fsdp'), may hold values from -1.75 to 1.75
- w_out: bfloat16 [768, 768], P('fsdp'), may hold values from -0.875 to 0.875
- b_out: bfloat16 [768], P('fsdp'), may hold values from -1.75 to 1.75
- ln2_gain: bfloat16 [768], P('fsdp'), may hold values from 0.5 to 1.5
- ln2_bias: bfloat16 [768], P('fsdp'), may hold values from -1.75 to 1.75
- w_up: bfloat16 [768, 3072], P('fsdp'), may hold values from -0.21875 to 0.21875
- b_up: bfloat16 [3072], P('fsdp'), may hold values from -1.75 to 1.75
- w_down: bfloat16 [3072, 768], P('fsdp'), may hold values from -0.109375 to 0.109375
- b_down: bfloat16 [768], P('fsdp'), may hold values from -1.75 to 1.75
- cotangent: bfloat16 [32768, 768], P('fsdp'), may hold values from -12 to 12
Outputs:
- output: bfloat16 [32768, 768], P('fsdp')
- grad_x: float32 [32768, 768], P('fsdp')
- grad_ln1_gain: float32 [768], P('fsdp')
- grad_ln1_bias: float32 [768], P('fsdp')
- grad_w_qkv: float32 [768, 2304], P('fsdp')
- grad_b_qv: float32 [1536], P('fsdp')
- grad_w_out: float32 [768, 768], P('fsdp')
- grad_b_out: float32 [768], P('fsdp')
- grad_ln2_gain: float32 [768], P('fsdp')
- grad_ln2_bias: float32 [768], P('fsdp')
- grad_w_up: float32 [768, 3072], P('fsdp')
- grad_b_up: float32 [3072], P('fsdp')
- grad_w_down: float32 [3072, 768], P('fsdp')
- grad_b_down: float32 [768], P('fsdp')
The draws below stay inside these ranges and needn't reach their ends.
Inputs may be any that keep to these rules, and one draw needn't show every extreme that they name: Device d's sequence fills the first lengths[d] of its 1024 slots. In every draw some device holds exactly 1024 tokens and some device exactly 512.
All inputs are finite; a program needn't handle non-finite values.
Results may differ from the reference program's by a relative error of at most 0.012.
The reference program's roundings to bfloat16 on the way count: a program that leaves them out, or rounds other values in their place, can miss the bound.
Values may be sent and summed in bfloat16 or wider, within the bound.
A program may use at most 256 MiB of HBM per device.

```python
import jax
import jax.numpy as jnp
from jax import lax

D = 768
HEADS = 12
HEAD_DIM = 64
FF = 3072
TOK_DEV = 1024
SEQS = 32
TOKENS = 32768


def draw_lengths(key, part):
    key = jax.random.fold_in(key, 11)
    least_len = TOK_DEV // 2
    most_len = TOK_DEV
    picked = jax.random.randint(jax.random.fold_in(key, 1), (SEQS,), least_len, most_len + 1, dtype=jnp.int32)
    shuffled = jax.random.permutation(jax.random.fold_in(key, 2), SEQS)
    picked = picked.at[shuffled[0]].set(most_len)
    picked = picked.at[shuffled[1]].set(least_len)
    return picked.astype(jnp.int32)


def strengthened(values, rng, source, target, shards_of, factor):
    def block_of(position):
        return (jnp.arange(values.shape[position]) // (values.shape[position] // shards_of)).reshape((-1,) + (1,) * (values.ndim - 1 - position))

    first = jax.random.permutation(rng, shards_of)[block_of(target)]
    far = (block_of(target) + shards_of // 2) % shards_of
    return jnp.where((block_of(source) == first) | (block_of(source) == far), factor * values, values)


def block_scale(stream_key, shape, cuts, least, largest):
    level, own = 1.0, jax.random.fold_in(stream_key, 6)
    for position, parts in cuts:
        heights = jnp.exp(jax.random.uniform(jax.random.fold_in(own, position), (parts,), jnp.float32, least / len(cuts), largest / len(cuts)))
        level = level * jnp.repeat(heights, shape[position] // parts).reshape([-1 if axis == position else 1 for axis in range(len(shape))])
    return level


def gaussian(stream_key, extent, deviation, limit, pieces=(), kind=jnp.bfloat16):
    drawn = jax.random.normal(stream_key, extent, jnp.float32) * deviation
    if len(pieces) > 0:
        drawn = block_scale(stream_key, extent, pieces, -0.22, 0.18) * drawn
    return jnp.clip(drawn, min=-limit, max=limit).astype(kind)


def bell_draw_with(stream_key, shape, width, bound, cuts, heavy, held_as=jnp.bfloat16):
    entries = width * jax.random.normal(stream_key, shape, jnp.float32)
    if cuts:
        entries = entries * block_scale(stream_key, shape, cuts, -0.22, 0.18)
    return jnp.clip(strengthened(entries, jax.random.fold_in(stream_key, 3), *heavy), -bound, bound).astype(held_as)


def setup_inputs(seed: int = 0) -> dict:
    arg_keys = jax.random.split(jax.random.key(seed), 16)
    return {
        "hidden_in": gaussian(arg_keys[0], (TOKENS, D), 1.0, 6.0, ((0, 32),)),
        "lengths": draw_lengths(jax.random.fold_in(arg_keys[15], 71), 0),
        "ln1_gain": jnp.clip(1.0 + 0.1 * jax.random.normal(arg_keys[2], (D,), jnp.float32), 0.5, 1.5).astype(jnp.bfloat16),
        "ln1_bias": gaussian(arg_keys[3], (D,), 0.3, 1.75, ((0, 32),)),
        "w_qkv": gaussian(arg_keys[4], (D, 3 * D), (D // 2) ** -0.5, 0.3125, ((0, 32),)),
        "b_qv": gaussian(arg_keys[5], (2 * D,), 0.3, 1.75, ((0, 32),)),
        "w_out": gaussian(arg_keys[6], (D, D), (D // 16) ** -0.5, 0.875, ((0, 32),)),
        "b_out": gaussian(arg_keys[7], (D,), 0.3, 1.75, ((0, 32),)),
        "ln2_gain": jnp.clip(1.0 + 0.1 * jax.random.normal(arg_keys[8], (D,), jnp.float32), 0.5, 1.5).astype(jnp.bfloat16),
        "ln2_bias": gaussian(arg_keys[9], (D,), 0.3, 1.75, ((0, 32),)),
        "w_up": gaussian(arg_keys[10], (D, FF), D ** -0.5, 0.21875, ((0, 32),)),
        "b_up": gaussian(arg_keys[11], (FF,), 0.3, 1.75, ((0, 32),)),
        "w_down": gaussian(arg_keys[12], (FF, D), FF ** -0.5, 0.109375, ((0, 32),)),
        "b_down": gaussian(arg_keys[13], (D,), 0.3, 1.75, ((0, 32),)),
        "cotangent": bell_draw_with(arg_keys[14], (TOKENS, D), 1.0, 12.0, ((0, 32),), (0, 1, 32, 2.75)),
    }


EPSILON = 1e-05
NEG_FILL = -1e+30

@jax.custom_vjp
def low(v):
    return lax.optimization_barrier(v.astype(jnp.bfloat16)).astype(jnp.float32)

@jax.custom_vjp
def low_back(v):
    return v

def low_keep(v):
    return (low(v), None)

def low_pass(kept, grad):
    return (grad,)

def back_keep(v):
    return (v, None)

def back_low(kept, grad):
    return (low(grad),)
low.defvjp(low_keep, low_pass)
low_back.defvjp(back_keep, back_low)

def normalize(values, gain_vec, shift_vec):
    row_mean = lax.optimization_barrier(jnp.mean(values, axis=-1, keepdims=True))
    centred = values - row_mean
    variance = lax.optimization_barrier(jnp.mean(centred * centred, axis=-1, keepdims=True))
    return centred * lax.rsqrt(variance + EPSILON) * gain_vec + shift_vec

def device_layer(block_in, seq_length, weights):
    gain_one, shift_one, qkv_weight, qv_bias, out_weight, out_bias, gain_two, shift_two, up_weight, up_bias, down_weight, down_bias = weights
    highest = lax.Precision.HIGHEST
    token_count = block_in.shape[0]
    positions = jnp.arange(token_count, dtype=jnp.int32)
    live_mask = (positions < seq_length).astype(jnp.float32)[:, None]
    segment = (positions >= seq_length).astype(jnp.int32)
    allowed = jnp.logical_and(segment[:, None] == segment[None, :], positions[None, :] <= positions[:, None])
    normed_one = low(normalize(block_in, gain_one, shift_one))
    bias_full = jnp.concatenate([qv_bias[:D], jnp.zeros((D,), jnp.float32), qv_bias[D:]])
    projected = low_back(low(jnp.dot(normed_one, qkv_weight, precision=highest) + bias_full))
    queries = projected[:, :D].reshape(token_count, HEADS, HEAD_DIM)
    keys = projected[:, D:2 * D].reshape(token_count, HEADS, HEAD_DIM)
    values = projected[:, 2 * D:].reshape(token_count, HEADS, HEAD_DIM)
    scores = low_back(jnp.einsum('qhd,khd->hqk', queries, keys, precision=highest) * HEAD_DIM ** (-0.5))
    scores = jnp.where(allowed[None], scores, NEG_FILL)
    row_top = lax.optimization_barrier(jnp.max(scores, axis=-1, keepdims=True))
    exp_scores = jnp.exp(scores - row_top)
    probs = low(exp_scores / lax.optimization_barrier(jnp.sum(exp_scores, axis=-1, keepdims=True)))
    attended = jnp.einsum('hqk,khd->qhd', probs, values, precision=highest).reshape(token_count, D)
    attended = low_back(low(attended))
    attn_out = low_back(jnp.dot(attended, out_weight, precision=highest) + out_bias)
    middle = block_in + attn_out
    normed_two = low(normalize(middle, gain_two, shift_two))
    hidden_pre = low_back(jnp.dot(normed_two, up_weight, precision=highest) + up_bias)
    activated = low(jax.nn.gelu(hidden_pre, approximate=True))
    mlp_out = low_back(jnp.dot(activated, down_weight, precision=highest) + down_bias)
    return live_mask * (middle + mlp_out)

def reference(hidden_in, lengths, ln1_gain, ln1_bias, w_qkv, b_qv, w_out, b_out, ln2_gain, ln2_bias, w_up, b_up, w_down, b_down, cotangent):

    def forward(inputs, gain_one, shift_one, qkv_weight, qv_bias, out_weight, out_bias, gain_two, shift_two, up_weight, up_bias, down_weight, down_bias):
        weights = (gain_one, shift_one, qkv_weight, qv_bias, out_weight, out_bias, gain_two, shift_two, up_weight, up_bias, down_weight, down_bias)

        def per_device(device_items):
            return device_layer(device_items[0], device_items[1], weights)
        blocks = inputs.reshape(SEQS, TOK_DEV, D)
        block_outs = lax.map(jax.checkpoint(per_device), (blocks, lengths.astype(jnp.int32)))
        return block_outs.reshape(TOKENS, D)
    result, pullback = jax.vjp(forward, hidden_in.astype(jnp.float32), ln1_gain.astype(jnp.float32), ln1_bias.astype(jnp.float32), w_qkv.astype(jnp.float32), b_qv.astype(jnp.float32), w_out.astype(jnp.float32), b_out.astype(jnp.float32), ln2_gain.astype(jnp.float32), ln2_bias.astype(jnp.float32), w_up.astype(jnp.float32), b_up.astype(jnp.float32), w_down.astype(jnp.float32), b_down.astype(jnp.float32))
    grads = pullback(cotangent.astype(jnp.float32))
    return (result.astype(jnp.bfloat16), grads[0], grads[1], grads[2], grads[3], grads[4], grads[5], grads[6], grads[7], grads[8], grads[9], grads[10], grads[11], grads[12])
```

```python
import functools

import jax
import jax.numpy as jnp
from jax import lax
from jax.experimental import pallas as pl
from jax.experimental.pallas import tpu as pltpu
from jax.sharding import PartitionSpec as P

HEAD_DIM = 64


EPSILON = 1e-05
NEG_FILL = -1e30


def normalize(values, gain_vec, shift_vec):
    row_mean = jnp.mean(values, axis=-1, keepdims=True)
    centred = values - row_mean
    variance = jnp.mean(centred * centred, axis=-1, keepdims=True)
    return centred * lax.rsqrt(variance + EPSILON) * gain_vec + shift_vec


def gelu_tanh(values):
    return jax.nn.gelu(values, approximate=True)


def weight_grad(left, right):
    return lax.dot_general(
        left, right, (((0,), (0,)), ((), ())), preferred_element_type=jnp.float32
    )


def back_product(grad_low, weight):
    return lax.dot_general(
        grad_low, weight, (((1,), (1,)), ((), ())), preferred_element_type=jnp.float32
    )


LANES = 128
NT = (((1,), (1,)), ((), ()))
TN = (((0,), (0,)), ((), ()))


def dot32(left, right, dims=(((1,), (0,)), ((), ()))):
    return lax.dot_general(left, right, dims, preferred_element_type=jnp.float32)


def head_masks(rows):
    lane = lax.broadcasted_iota(jnp.int32, (rows, LANES), 1)
    return lane < HEAD_DIM


def pick(mask, array, head):
    zero = jnp.zeros_like(array)
    return jnp.where(mask, array, zero) if head == 0 else jnp.where(mask, zero, array)


def attend_kernel(block, q_ref, k_ref, v_ref, out_ref, lse_ref):
    rows = q_ref.shape[0]
    scale_value = HEAD_DIM ** (-0.5)
    mask = head_masks(rows)
    keys = k_ref[...]
    values = v_ref[...]
    keys_of = [pick(mask, keys, head) for head in range(2)]
    values_of = [pick(mask, values, head) for head in range(2)]
    for start in range(0, rows, block):
        stop = start + block
        queries = q_ref[start:stop, :] * jnp.bfloat16(scale_value)
        total = None
        for head in range(2):
            scores = dot32(queries, keys_of[head][:stop], NT)
            row = lax.broadcasted_iota(jnp.int32, scores.shape, 0) + start
            column = lax.broadcasted_iota(jnp.int32, scores.shape, 1)
            scores = jnp.where(column <= row, scores, NEG_FILL)
            row_top = jnp.max(scores, axis=-1, keepdims=True)
            exp_scores = jnp.exp(scores - row_top)
            row_total = jnp.sum(exp_scores, axis=-1, keepdims=True)
            probs_low = (exp_scores * (1.0 / row_total)).astype(jnp.bfloat16)
            part = dot32(probs_low, values_of[head][:stop])
            total = part if total is None else total + part
            lse = jnp.broadcast_to(row_top + jnp.log(row_total), (block, LANES))
            lse_ref[0, head : head + 1, start:stop] = lse.T[:1]
        out_ref[start:stop, :] = total.astype(jnp.bfloat16)


def attend_back_kernel(
    block, q_ref, k_ref, v_ref, out_ref, lse_ref, grad_ref, dq_ref, dk_ref, dv_ref, dk_sum, dv_sum
):
    rows = q_ref.shape[0]
    scale_value = HEAD_DIM ** (-0.5)
    mask = head_masks(rows)
    keys = k_ref[...]
    values = v_ref[...]
    keys_of = [pick(mask, keys, head) for head in range(2)]
    values_of = [pick(mask, values, head) for head in range(2)]
    dk_sum[...] = jnp.zeros_like(dk_sum)
    dv_sum[...] = jnp.zeros_like(dv_sum)
    for start in range(0, rows, block):
        stop = start + block
        queries = q_ref[start:stop, :] * jnp.bfloat16(scale_value)
        grad = grad_ref[start:stop, :]
        turned = (grad.astype(jnp.float32) * out_ref[start:stop, :].astype(jnp.float32)).T
        grad_q = None
        for head in range(2):
            row_delta = jnp.sum(
                turned[head * HEAD_DIM : (head + 1) * HEAD_DIM], axis=0, keepdims=True
            )
            lse = lse_ref[0, head : head + 1, start:stop]
            scores = dot32(keys_of[head][:stop], queries, NT)
            key_pos = lax.broadcasted_iota(jnp.int32, scores.shape, 0)
            query_pos = lax.broadcasted_iota(jnp.int32, scores.shape, 1) + start
            probs = jnp.where(key_pos <= query_pos, jnp.exp(scores - lse), 0.0)
            grad_probs = dot32(values_of[head][:stop], grad, NT)
            grad_scores = (probs * (grad_probs - row_delta)).astype(jnp.bfloat16)
            dv_sum[:stop, :] += dot32(probs.astype(jnp.bfloat16), pick(mask[:block], grad, head))
            dk_sum[:stop, :] += dot32(grad_scores, pick(mask[:block], queries, head))
            part = dot32(grad_scores, keys_of[head][:stop], TN)
            grad_q = part if grad_q is None else grad_q + part
        dq_ref[start:stop, :] = (grad_q * scale_value).astype(jnp.bfloat16)
    dk_ref[...] = dk_sum[...].astype(jnp.bfloat16)
    dv_ref[...] = dv_sum[...].astype(jnp.bfloat16)


def column_spec(rows, offset):
    return pl.BlockSpec((rows, LANES), lambda pair: (0, offset + pair))


def lse_spec(rows):
    return pl.BlockSpec((1, 8, rows), lambda pair: (pair, 0, 0))


def attend(qkv_low):
    rows, width = qkv_low.shape[0], qkv_low.shape[1] // 3
    pairs = width // LANES
    block = min(256, rows)
    return pl.pallas_call(
        functools.partial(attend_kernel, block),
        grid=(pairs,),
        in_specs=[column_spec(rows, pairs * part) for part in range(3)],
        out_specs=[column_spec(rows, 0), lse_spec(rows)],
        out_shape=[
            jax.ShapeDtypeStruct((rows, width), jnp.bfloat16),
            jax.ShapeDtypeStruct((pairs, 8, rows), jnp.float32),
        ],
        compiler_params=pltpu.CompilerParams(vmem_limit_bytes=40 * 1024 * 1024),
        cost_estimate=pl.CostEstimate(
            flops=4 * rows * rows * width, bytes_accessed=8 * rows * width, transcendentals=0
        ),
    )(qkv_low, qkv_low, qkv_low)


def attend_back(qkv_low, attended, lse, grad_attended):
    rows, width = attended.shape
    pairs = width // LANES
    block = min(256, rows)
    return pl.pallas_call(
        functools.partial(attend_back_kernel, block),
        grid=(pairs,),
        in_specs=[column_spec(rows, pairs * part) for part in range(3)]
        + [column_spec(rows, 0), lse_spec(rows), column_spec(rows, 0)],
        out_specs=[column_spec(rows, 0)] * 3,
        out_shape=[jax.ShapeDtypeStruct((rows, width), jnp.bfloat16)] * 3,
        scratch_shapes=[pltpu.VMEM((rows, LANES), jnp.float32)] * 2,
        compiler_params=pltpu.CompilerParams(vmem_limit_bytes=40 * 1024 * 1024),
        cost_estimate=pl.CostEstimate(
            flops=10 * rows * rows * width, bytes_accessed=16 * rows * width, transcendentals=0
        ),
    )(qkv_low, qkv_low, qkv_low, attended, lse, grad_attended)


def fold(shard, width):
    rows, columns = shard.shape
    return shard.reshape(rows, columns // width, width).transpose(1, 0, 2).reshape(-1, width)


def unfold(stacked, count):
    parts, rows, width = stacked.shape
    each = rows // count
    return (
        stacked.reshape(parts, count, each, width)
        .transpose(0, 2, 1, 3)
        .reshape(parts * each, count * width)
    )


def fold_all(full, parts, width):
    rows = full.shape[0] // parts
    count = full.shape[1] // width
    return (
        full.reshape(parts, rows, count, width)
        .transpose(0, 2, 1, 3)
        .reshape(parts, count * rows, width)
    )


def unfold_one(stacked, count):
    return unfold(stacked[None], count)


def local(
    hidden_in,
    lengths,
    ln1_gain,
    ln1_bias,
    w_qkv,
    b_qv,
    w_out,
    b_out,
    ln2_gain,
    ln2_bias,
    w_up,
    b_up,
    w_down,
    b_down,
    cotangent,
):
    token_count = hidden_in.shape[0]
    model_width = hidden_in.shape[1]
    parts = lax.axis_size("fsdp")
    vectors = (ln1_gain, ln1_bias, b_qv, b_out, ln2_gain, ln2_bias, b_up, b_down)
    joined = jnp.concatenate(vectors)
    vector_rows = 16
    vector_pad = jnp.zeros((vector_rows, model_width), jnp.bfloat16)
    vector_block = lax.dynamic_update_slice(vector_pad, joined[None], (0, 0))
    own_rows = w_qkv.shape[0]

    def gathered(pieces):
        stacked = jnp.concatenate(pieces, axis=0)
        whole = lax.all_gather(stacked, "fsdp", axis=0, tiled=True)
        return whole.reshape(parts, stacked.shape[0], model_width)

    first = gathered([fold(w_qkv, model_width), vector_block])
    qkv_rows = 3 * own_rows
    qkv_weight = unfold(first[:, :qkv_rows], 3)
    full_vectors = []
    offset = 0
    for vector in vectors:
        size = vector.shape[0]
        full_vectors.append(
            first[:, qkv_rows, offset : offset + size].reshape(-1).astype(jnp.float32)
        )
        offset += size
    gain_one, shift_one, qv_bias, out_bias, gain_two, shift_two, up_bias, down_bias = full_vectors
    up_count = w_up.shape[1] // model_width
    second = gathered([w_out, fold(w_up, model_width), w_down])
    out_weight = second[:, :own_rows].reshape(-1, model_width)
    up_rows = own_rows * up_count
    up_weight = unfold(second[:, own_rows : own_rows + up_rows], up_count)
    down_weight = second[:, own_rows + up_rows :].reshape(-1, model_width)

    positions = jnp.arange(token_count, dtype=jnp.int32)
    live_mask = (positions < lengths[0]).astype(jnp.float32)[:, None]
    inputs = hidden_in.astype(jnp.float32)
    normed_one, norm_one_back = jax.vjp(normalize, inputs, gain_one, shift_one)
    normed_one = normed_one.astype(jnp.bfloat16)
    bias_full = jnp.concatenate(
        [qv_bias[:model_width], jnp.zeros((model_width,), jnp.float32), qv_bias[model_width:]]
    )
    qkv_low = (
        jnp.dot(normed_one, qkv_weight, preferred_element_type=jnp.float32) + bias_full
    ).astype(jnp.bfloat16)
    attended, lse = attend(qkv_low)
    middle = inputs + (
        jnp.dot(attended, out_weight, preferred_element_type=jnp.float32) + out_bias
    )
    normed_two, norm_two_back = jax.vjp(normalize, middle, gain_two, shift_two)
    normed_two = normed_two.astype(jnp.bfloat16)
    hidden_pre = jnp.dot(normed_two, up_weight, preferred_element_type=jnp.float32) + up_bias
    activated = gelu_tanh(hidden_pre).astype(jnp.bfloat16)
    mlp_out = jnp.dot(activated, down_weight, preferred_element_type=jnp.float32) + down_bias
    output = (live_mask * (middle + mlp_out)).astype(jnp.bfloat16)

    grad_out = cotangent.astype(jnp.float32) * live_mask
    grad_out_low = grad_out.astype(jnp.bfloat16)
    grad_w_down = weight_grad(activated, grad_out_low).astype(jnp.bfloat16)
    grad_b_down = jnp.sum(grad_out, axis=0)
    grad_act = back_product(grad_out_low, down_weight)
    gelu_back = jax.vjp(gelu_tanh, hidden_pre)[1]
    grad_hidden = gelu_back(grad_act)[0].astype(jnp.bfloat16)
    grad_w_up = weight_grad(normed_two, grad_hidden).astype(jnp.bfloat16)
    grad_b_up = jnp.sum(grad_hidden.astype(jnp.float32), axis=0)

    def scattered(pieces):
        stacked = jnp.concatenate(pieces, axis=1)
        flat = stacked.reshape(-1, model_width)
        return lax.psum_scatter(flat, "fsdp", scatter_dimension=0, tiled=True)

    mlp_shard = scattered(
        [
            fold_all(grad_w_up, parts, model_width),
            grad_w_down.reshape(parts, -1, model_width),
        ]
    ).astype(jnp.float32)

    grad_middle_norm, grad_ln2_gain, grad_ln2_bias = norm_two_back(
        back_product(grad_hidden, up_weight)
    )
    grad_middle = grad_out + grad_middle_norm
    grad_attn_low = grad_middle.astype(jnp.bfloat16)
    grad_w_out = weight_grad(attended, grad_attn_low).astype(jnp.bfloat16)
    grad_b_out = jnp.sum(grad_attn_low.astype(jnp.float32), axis=0)
    grad_attended = back_product(grad_attn_low, out_weight).astype(jnp.bfloat16)
    grad_parts = attend_back(qkv_low, attended, lse, grad_attended)
    grad_qkv = jnp.concatenate(grad_parts, axis=1)
    grad_w_qkv = [weight_grad(normed_one, part).astype(jnp.bfloat16) for part in grad_parts]
    grad_b_qv = jnp.concatenate(
        [
            jnp.sum(grad_parts[0].astype(jnp.float32), axis=0),
            jnp.sum(grad_parts[2].astype(jnp.float32), axis=0),
        ]
    )
    grad_in_norm, grad_ln1_gain, grad_ln1_bias = norm_one_back(
        back_product(grad_qkv, qkv_weight)
    )
    grad_inputs = grad_middle + grad_in_norm
    vector_grads = (
        grad_ln1_gain,
        grad_ln1_bias,
        grad_b_qv,
        grad_b_out,
        grad_ln2_gain,
        grad_ln2_bias,
        grad_b_up,
        grad_b_down,
    )
    vector_rows_grad = jnp.concatenate([g.reshape(parts, -1) for g in vector_grads], axis=1)
    vector_rows_grad = vector_rows_grad.astype(jnp.bfloat16)[:, None, :]
    padded = jnp.pad(
        vector_rows_grad,
        ((0, 0), (0, vector_rows - 1), (0, model_width - vector_rows_grad.shape[2])),
    )
    attn_shard = scattered(
        [part.reshape(parts, -1, model_width) for part in grad_w_qkv]
        + [grad_w_out.reshape(parts, -1, model_width), padded]
    ).astype(jnp.float32)
    grad_vector_shards = []
    offset = 0
    for vector in vectors:
        size = vector.shape[0]
        grad_vector_shards.append(attn_shard[4 * own_rows, offset : offset + size])
        offset += size
    g_ln1g, g_ln1b, g_bqv, g_bout, g_ln2g, g_ln2b, g_bup, g_bdown = grad_vector_shards
    return (
        output,
        grad_inputs,
        g_ln1g,
        g_ln1b,
        unfold_one(attn_shard[:qkv_rows], 3),
        g_bqv,
        attn_shard[qkv_rows : qkv_rows + own_rows],
        g_bout,
        g_ln2g,
        g_ln2b,
        unfold_one(mlp_shard[:up_rows], up_count),
        g_bup,
        mlp_shard[up_rows:],
        g_bdown,
    )


def solution(mesh):
    return jax.shard_map(
        local,
        mesh=mesh,
        in_specs=(
            P("fsdp", None),
            P("fsdp"),
            P("fsdp"),
            P("fsdp"),
            P("fsdp", None),
            P("fsdp"),
            P("fsdp", None),
            P("fsdp"),
            P("fsdp"),
            P("fsdp"),
            P("fsdp", None),
            P("fsdp"),
            P("fsdp", None),
            P("fsdp"),
            P("fsdp", None),
        ),
        out_specs=(
            P("fsdp", None),
            P("fsdp", None),
            P("fsdp"),
            P("fsdp"),
            P("fsdp", None),
            P("fsdp"),
            P("fsdp", None),
            P("fsdp"),
            P("fsdp"),
            P("fsdp"),
            P("fsdp", None),
            P("fsdp"),
            P("fsdp", None),
            P("fsdp"),
        ),
        check_vma=False,
    )
```

```python
import functools

import jax
import jax.numpy as jnp
from jax import lax
from jax.experimental import pallas as pl
from jax.experimental.pallas import tpu as pltpu
from jax.sharding import PartitionSpec as P

HEAD_DIM = 64


EPSILON = 1e-05
NEG_FILL = -1e30


def normalize(values, gain_vec, shift_vec):
    row_mean = jnp.mean(values, axis=-1, keepdims=True)
    centred = values - row_mean
    variance = jnp.mean(centred * centred, axis=-1, keepdims=True)
    return centred * lax.rsqrt(variance + EPSILON) * gain_vec + shift_vec


def gelu_tanh(values):
    return jax.nn.gelu(values, approximate=True)


def weight_grad(left, right):
    return lax.dot_general(
        left, right, (((0,), (0,)), ((), ())), preferred_element_type=jnp.float32
    )


def back_product(grad_low, weight):
    return lax.dot_general(
        grad_low, weight, (((1,), (1,)), ((), ())), preferred_element_type=jnp.float32
    )


LANES = 128
NT = (((1,), (1,)), ((), ()))
TN = (((0,), (0,)), ((), ()))


def dot32(left, right, dims=(((1,), (0,)), ((), ()))):
    return lax.dot_general(left, right, dims, preferred_element_type=jnp.float32)


def head_masks(rows):
    lane = lax.broadcasted_iota(jnp.int32, (rows, LANES), 1)
    return lane < HEAD_DIM


def pick(mask, array, head):
    zero = jnp.zeros_like(array)
    return jnp.where(mask, array, zero) if head == 0 else jnp.where(mask, zero, array)


def attend_kernel(block, q_ref, k_ref, v_ref, out_ref, lse_ref):
    rows = q_ref.shape[0]
    scale_value = HEAD_DIM ** (-0.5)
    mask = head_masks(rows)
    keys = k_ref[...]
    values = v_ref[...]
    keys_of = [pick(mask, keys, head) for head in range(2)]
    values_of = [pick(mask, values, head) for head in range(2)]
    for start in range(0, rows, block):
        stop = start + block
        queries = q_ref[start:stop, :] * jnp.bfloat16(scale_value)
        total = None
        for head in range(2):
            scores = dot32(queries, keys_of[head][:stop], NT)
            row = lax.broadcasted_iota(jnp.int32, scores.shape, 0) + start
            column = lax.broadcasted_iota(jnp.int32, scores.shape, 1)
            scores = jnp.where(column <= row, scores, NEG_FILL)
            row_top = jnp.max(scores, axis=-1, keepdims=True)
            exp_scores = jnp.exp(scores - row_top)
            row_total = jnp.sum(exp_scores, axis=-1, keepdims=True)
            probs_low = (exp_scores * (1.0 / row_total)).astype(jnp.bfloat16)
            part = dot32(probs_low, values_of[head][:stop])
            total = part if total is None else total + part
            lse = jnp.broadcast_to(row_top + jnp.log(row_total), (block, LANES))
            lse_ref[0, head : head + 1, start:stop] = lse.T[:1]
        out_ref[start:stop, :] = total.astype(jnp.bfloat16)


def attend_back_kernel(
    block, q_ref, k_ref, v_ref, out_ref, lse_ref, grad_ref, dq_ref, dk_ref, dv_ref, dk_sum, dv_sum
):
    rows = q_ref.shape[0]
    scale_value = HEAD_DIM ** (-0.5)
    mask = head_masks(rows)
    keys = k_ref[...]
    values = v_ref[...]
    keys_of = [pick(mask, keys, head) for head in range(2)]
    values_of = [pick(mask, values, head) for head in range(2)]
    dk_sum[...] = jnp.zeros_like(dk_sum)
    dv_sum[...] = jnp.zeros_like(dv_sum)
    for start in range(0, rows, block):
        stop = start + block
        queries = q_ref[start:stop, :] * jnp.bfloat16(scale_value)
        grad = grad_ref[start:stop, :]
        turned = (grad.astype(jnp.float32) * out_ref[start:stop, :].astype(jnp.float32)).T
        grad_q = None
        for head in range(2):
            row_delta = jnp.sum(
                turned[head * HEAD_DIM : (head + 1) * HEAD_DIM], axis=0, keepdims=True
            )
            lse = lse_ref[0, head : head + 1, start:stop]
            scores = dot32(keys_of[head][:stop], queries, NT)
            key_pos = lax.broadcasted_iota(jnp.int32, scores.shape, 0)
            query_pos = lax.broadcasted_iota(jnp.int32, scores.shape, 1) + start
            probs = jnp.where(key_pos <= query_pos, jnp.exp(scores - lse), 0.0)
            grad_probs = dot32(values_of[head][:stop], grad, NT)
            grad_scores = (probs * (grad_probs - row_delta)).astype(jnp.bfloat16)
            dv_sum[:stop, :] += dot32(probs.astype(jnp.bfloat16), pick(mask[:block], grad, head))
            dk_sum[:stop, :] += dot32(grad_scores, pick(mask[:block], queries, head))
            part = dot32(grad_scores, keys_of[head][:stop], TN)
            grad_q = part if grad_q is None else grad_q + part
        dq_ref[start:stop, :] = (grad_q * scale_value).astype(jnp.bfloat16)
    dk_ref[...] = dk_sum[...].astype(jnp.bfloat16)
    dv_ref[...] = dv_sum[...].astype(jnp.bfloat16)


def column_spec(rows, offset):
    return pl.BlockSpec((rows, LANES), lambda pair: (0, offset + pair))


def lse_spec(rows):
    return pl.BlockSpec((1, 8, rows), lambda pair: (pair, 0, 0))


def attend(qkv_low):
    rows, width = qkv_low.shape[0], qkv_low.shape[1] // 3
    pairs = width // LANES
    block = min(256, rows)
    return pl.pallas_call(
        functools.partial(attend_kernel, block),
        grid=(pairs,),
        in_specs=[column_spec(rows, pairs * part) for part in range(3)],
        out_specs=[column_spec(rows, 0), lse_spec(rows)],
        out_shape=[
            jax.ShapeDtypeStruct((rows, width), jnp.bfloat16),
            jax.ShapeDtypeStruct((pairs, 8, rows), jnp.float32),
        ],
        compiler_params=pltpu.CompilerParams(vmem_limit_bytes=40 * 1024 * 1024),
        cost_estimate=pl.CostEstimate(
            flops=4 * rows * rows * width, bytes_accessed=8 * rows * width, transcendentals=0
        ),
    )(qkv_low, qkv_low, qkv_low)


def attend_back(qkv_low, attended, lse, grad_attended):
    rows, width = attended.shape
    pairs = width // LANES
    block = min(256, rows)
    return pl.pallas_call(
        functools.partial(attend_back_kernel, block),
        grid=(pairs,),
        in_specs=[column_spec(rows, pairs * part) for part in range(3)]
        + [column_spec(rows, 0), lse_spec(rows), column_spec(rows, 0)],
        out_specs=[column_spec(rows, 0)] * 3,
        out_shape=[jax.ShapeDtypeStruct((rows, width), jnp.bfloat16)] * 3,
        scratch_shapes=[pltpu.VMEM((rows, LANES), jnp.float32)] * 2,
        compiler_params=pltpu.CompilerParams(vmem_limit_bytes=40 * 1024 * 1024),
        cost_estimate=pl.CostEstimate(
            flops=10 * rows * rows * width, bytes_accessed=16 * rows * width, transcendentals=0
        ),
    )(qkv_low, qkv_low, qkv_low, attended, lse, grad_attended)


def fold(shard, width):
    rows, columns = shard.shape
    return shard.reshape(rows, columns // width, width).transpose(1, 0, 2).reshape(-1, width)


def unfold(stacked, count):
    parts, rows, width = stacked.shape
    each = rows // count
    return (
        stacked.reshape(parts, count, each, width)
        .transpose(0, 2, 1, 3)
        .reshape(parts * each, count * width)
    )


def unfold_one(stacked, count):
    return unfold(stacked[None], count)


def local(
    hidden_in,
    lengths,
    ln1_gain,
    ln1_bias,
    w_qkv,
    b_qv,
    w_out,
    b_out,
    ln2_gain,
    ln2_bias,
    w_up,
    b_up,
    w_down,
    b_down,
    cotangent,
):
    token_count = hidden_in.shape[0]
    model_width = hidden_in.shape[1]
    parts = lax.axis_size("fsdp")
    vectors = (ln1_gain, ln1_bias, b_qv, b_out, ln2_gain, ln2_bias, b_up, b_down)
    joined = jnp.concatenate(vectors)
    vector_rows = 16
    vector_pad = jnp.zeros((vector_rows, model_width), jnp.bfloat16)
    vector_block = lax.dynamic_update_slice(vector_pad, joined[None], (0, 0))
    own_rows = w_qkv.shape[0]

    def gathered(pieces):
        stacked = jnp.concatenate(pieces, axis=0)
        whole = lax.all_gather(stacked, "fsdp", axis=0, tiled=True)
        return whole.reshape(parts, stacked.shape[0], model_width)

    first = gathered([fold(w_qkv, model_width), vector_block])
    qkv_rows = 3 * own_rows
    qkv_weight = unfold(first[:, :qkv_rows], 3)
    full_vectors = []
    offset = 0
    for vector in vectors:
        size = vector.shape[0]
        full_vectors.append(
            first[:, qkv_rows, offset : offset + size].reshape(-1).astype(jnp.float32)
        )
        offset += size
    gain_one, shift_one, qv_bias, out_bias, gain_two, shift_two, up_bias, down_bias = full_vectors
    up_count = w_up.shape[1] // model_width
    second = gathered([w_out, fold(w_up, model_width), w_down])
    out_weight = second[:, :own_rows].reshape(-1, model_width)
    up_rows = own_rows * up_count
    up_weight = unfold(second[:, own_rows : own_rows + up_rows], up_count)
    down_weight = second[:, own_rows + up_rows :].reshape(-1, model_width)

    positions = jnp.arange(token_count, dtype=jnp.int32)
    live_mask = (positions < lengths[0]).astype(jnp.float32)[:, None]
    inputs = hidden_in.astype(jnp.float32)
    normed_one, norm_one_back = jax.vjp(normalize, inputs, gain_one, shift_one)
    normed_one = normed_one.astype(jnp.bfloat16)
    bias_full = jnp.concatenate(
        [qv_bias[:model_width], jnp.zeros((model_width,), jnp.float32), qv_bias[model_width:]]
    )
    qkv_low = (
        jnp.dot(normed_one, qkv_weight, preferred_element_type=jnp.float32) + bias_full
    ).astype(jnp.bfloat16)
    attended, lse = attend(qkv_low)
    middle = inputs + (
        jnp.dot(attended, out_weight, preferred_element_type=jnp.float32) + out_bias
    )
    normed_two, norm_two_back = jax.vjp(normalize, middle, gain_two, shift_two)
    normed_two = normed_two.astype(jnp.bfloat16)
    hidden_pre = jnp.dot(normed_two, up_weight, preferred_element_type=jnp.float32) + up_bias
    activated = gelu_tanh(hidden_pre).astype(jnp.bfloat16)
    mlp_out = jnp.dot(activated, down_weight, preferred_element_type=jnp.float32) + down_bias
    output = (live_mask * (middle + mlp_out)).astype(jnp.bfloat16)

    grad_out = cotangent.astype(jnp.float32) * live_mask
    grad_out_low = grad_out.astype(jnp.bfloat16)
    grad_w_down = weight_grad(activated, grad_out_low).astype(jnp.bfloat16)
    grad_b_down = jnp.sum(grad_out, axis=0)
    grad_act = back_product(grad_out_low, down_weight)
    gelu_back = jax.vjp(gelu_tanh, hidden_pre)[1]
    grad_hidden = gelu_back(grad_act)[0].astype(jnp.bfloat16)
    grad_w_up = [
        weight_grad(
            normed_two, grad_hidden[:, index * model_width : (index + 1) * model_width]
        ).astype(jnp.bfloat16)
        for index in range(up_count)
    ]
    grad_b_up = jnp.sum(grad_hidden.astype(jnp.float32), axis=0)

    def packed(pieces):
        return jnp.concatenate(pieces, axis=1).reshape(-1, model_width)

    def scattered(flat):
        return lax.psum_scatter(flat, "fsdp", scatter_dimension=0, tiled=True)

    mlp_packed = packed(
        [part.reshape(parts, -1, model_width) for part in grad_w_up]
        + [grad_w_down.reshape(parts, -1, model_width)]
    )
    mlp_packed, grad_hidden = lax.optimization_barrier((mlp_packed, grad_hidden))
    mlp_shard = scattered(mlp_packed).astype(jnp.float32)

    grad_middle_norm, grad_ln2_gain, grad_ln2_bias = norm_two_back(
        back_product(grad_hidden, up_weight)
    )
    grad_middle = grad_out + grad_middle_norm
    grad_attn_low = grad_middle.astype(jnp.bfloat16)
    grad_w_out = weight_grad(attended, grad_attn_low).astype(jnp.bfloat16)
    grad_b_out = jnp.sum(grad_attn_low.astype(jnp.float32), axis=0)
    grad_attended = back_product(grad_attn_low, out_weight).astype(jnp.bfloat16)
    grad_parts = attend_back(qkv_low, attended, lse, grad_attended)
    grad_qkv = jnp.concatenate(grad_parts, axis=1)
    grad_w_qkv = [weight_grad(normed_one, part).astype(jnp.bfloat16) for part in grad_parts]
    grad_b_qv = jnp.concatenate(
        [
            jnp.sum(grad_parts[0].astype(jnp.float32), axis=0),
            jnp.sum(grad_parts[2].astype(jnp.float32), axis=0),
        ]
    )
    grad_in_norm, grad_ln1_gain, grad_ln1_bias = norm_one_back(
        back_product(grad_qkv, qkv_weight)
    )
    grad_inputs = grad_middle + grad_in_norm
    vector_grads = (
        grad_ln1_gain,
        grad_ln1_bias,
        grad_b_qv,
        grad_b_out,
        grad_ln2_gain,
        grad_ln2_bias,
        grad_b_up,
        grad_b_down,
    )
    vector_rows_grad = jnp.concatenate([g.reshape(parts, -1) for g in vector_grads], axis=1)
    vector_rows_grad = vector_rows_grad.astype(jnp.bfloat16)[:, None, :]
    padded = jnp.pad(
        vector_rows_grad,
        ((0, 0), (0, vector_rows - 1), (0, model_width - vector_rows_grad.shape[2])),
    )
    attn_packed = packed(
        [part.reshape(parts, -1, model_width) for part in grad_w_qkv]
        + [grad_w_out.reshape(parts, -1, model_width), padded]
    )
    attn_shard = scattered(attn_packed).astype(jnp.float32)
    grad_vector_shards = []
    offset = 0
    for vector in vectors:
        size = vector.shape[0]
        grad_vector_shards.append(attn_shard[4 * own_rows, offset : offset + size])
        offset += size
    g_ln1g, g_ln1b, g_bqv, g_bout, g_ln2g, g_ln2b, g_bup, g_bdown = grad_vector_shards
    return (
        output,
        grad_inputs,
        g_ln1g,
        g_ln1b,
        unfold_one(attn_shard[:qkv_rows], 3),
        g_bqv,
        attn_shard[qkv_rows : qkv_rows + own_rows],
        g_bout,
        g_ln2g,
        g_ln2b,
        unfold_one(mlp_shard[:up_rows], up_count),
        g_bup,
        mlp_shard[up_rows:],
        g_bdown,
    )


def solution(mesh):
    return jax.shard_map(
        local,
        mesh=mesh,
        in_specs=(
            P("fsdp", None),
            P("fsdp"),
            P("fsdp"),
            P("fsdp"),
            P("fsdp", None),
            P("fsdp"),
            P("fsdp", None),
            P("fsdp"),
            P("fsdp"),
            P("fsdp"),
            P("fsdp", None),
            P("fsdp"),
            P("fsdp", None),
            P("fsdp"),
            P("fsdp", None),
        ),
        out_specs=(
            P("fsdp", None),
            P("fsdp", None),
            P("fsdp"),
            P("fsdp"),
            P("fsdp", None),
            P("fsdp"),
            P("fsdp", None),
            P("fsdp"),
            P("fsdp"),
            P("fsdp"),
            P("fsdp", None),
            P("fsdp"),
            P("fsdp", None),
            P("fsdp"),
        ),
        check_vma=False,
    )
```
